512 devices in a mesh: dp: 32 (over y, x_lo, core), mp: 16 (over x_hi, z).
Axes of the slice: x: 4 (x_hi: 2, x_lo: 2; x = x_hi * 2 + x_lo), y: 8, z: 8, core: 2. Of those that a mesh axis runs over, the one named last changes fastest.
Arguments:
- tokens: bfloat16 [8192, 2560], P('dp', 'mp'), may hold values from -6 to 6
- cotangent: bfloat16 [8192, 2560], P('dp', 'mp'), may hold values from -130085.49 to 130085.49
- gate_weight: bfloat16 [2560, 6912], P('dp', 'mp'), may hold values from -0.125 to 0.125
- up_weight: bfloat16 [2560, 6912], P('dp', 'mp'), may hold values from -5.9885633 to 5.9885633
- probe_gate: bfloat16 [2560, 6912], P('dp', 'mp'), may hold values from -6 to 6
- probe_up: bfloat16 [2560, 6912], P('dp', 'mp'), may hold values from -6 to 6
- probe_down: bfloat16 [2560, 6912], P('dp', 'mp'), may hold values from -6 to 6
- moment: float32 [2560, 6912], P('dp', 'mp'), may hold values from -0.12 to 0.12
- curvature: float32 [2560, 6912], P('dp', 'mp'), may hold values from 0.2 to 2
- step_count: int32 [], replicated, may hold values from 1 to 63
Outputs:
- moment_next: float32 [2560, 6912], P('dp', 'mp')
- curvature_next: float32 [2560, 6912], P('dp', 'mp')
- direction: bfloat16 [2560, 6912], P('dp', 'mp')
The draws below stay inside these ranges and needn't reach their ends.
Inputs may be any that keep to these rules, and one draw needn't show every extreme that they name: `step_count`: the number of optimizer steps taken, this one included, within the first steps after a restart.
All inputs are finite; a program needn't handle non-finite values.
Results may differ from the reference program's by a relative error of at most 0.04.
Values may be sent and summed in bfloat16 or wider, within the bound.
No kernel may reach another device: no remote copies, remote signals or barrier semaphores. Data moves between devices by JAX's collectives and lax.ppermute only.
A program may use at most 64 MiB of HBM per device.

```python
import math
import jax
import jax.numpy as jnp
from jax import lax

DW = 2560
FFW = 6912
TOK_DEV = 256
TOKENS = 8192


def ranked_scales(key, count, jitter_top, peak):
    order_key, jitter_key = jax.random.split(key, 2)
    rank_value = (jax.random.permutation(order_key, count) + 1).astype(jnp.float32)
    jitter = jnp.exp(jax.random.uniform(jitter_key, (count,), jnp.float32, 0.0, math.log(jitter_top)))
    return jitter + peak / (rank_value * rank_value)


def draw_cotangent(key, part):
    key = jax.random.fold_in(key, 11)
    scale_key, value_key = jax.random.split(key, 2)
    spread = 60.0 * (TOKENS / DW) ** 0.5
    scales = ranked_scales(scale_key, DW, 3.0, 300.0)
    values = jax.random.truncated_normal(value_key, -4.0, 4.0, (TOKENS, DW), jnp.float32)
    return (values * scales[None, :] * spread).astype(jnp.bfloat16)


def draw_up_weight(key, part):
    key = jax.random.fold_in(key, 12)
    scale_key, value_key = jax.random.split(key, 2)
    scales = ranked_scales(scale_key, FFW, 3.0, 300.0)
    values = jax.random.truncated_normal(value_key, -4.0, 4.0, (DW, FFW), jnp.float32)
    return (values * scales[None, :] * 0.25 / DW ** 0.5).astype(jnp.bfloat16)


def levels(rng, extent, cuts, least, largest):
    gain = 1.0
    for position, parts in cuts:
        steps = jax.random.uniform(jax.random.fold_in(jax.random.fold_in(rng, 6), position), (parts,), jnp.float32, least / len(cuts), largest / len(cuts))
        gain = gain * jnp.repeat(jnp.exp(steps), extent[position] // parts).reshape((-1,) + (1,) * (len(extent) - 1 - position))
    return gain


def scatter_about(stream_key, extent, scale, limit, cuts=(), dtype=jnp.bfloat16):
    drawn = jax.random.normal(stream_key, extent, jnp.float32) * scale
    if len(cuts) > 0:
        drawn = levels(stream_key, extent, cuts, -0.22, 0.18) * drawn
    return jnp.clip(drawn, min=-limit, max=limit).astype(dtype)


def setup_inputs(seed: int = 0) -> dict:
    keys = jax.random.split(jax.random.key(seed), 11)
    tokens = scatter_about(keys[0], (TOKENS, DW), 1.0, 6.0, ((0, 32), (1, 16)))
    cotangent = draw_cotangent(jax.random.fold_in(keys[10], 71), 0)
    gate_weight = scatter_about(keys[2], (DW, FFW), DW ** -0.5, 0.125, ((0, 32), (1, 16)))
    up_weight = draw_up_weight(jax.random.fold_in(keys[10], 71), 0)
    probe_gate = scatter_about(keys[4], (DW, FFW), 1.0, 6.0, ((0, 32), (1, 16)))
    probe_up = scatter_about(keys[5], (DW, FFW), 1.0, 6.0, ((0, 32), (1, 16)))
    probe_down = scatter_about(keys[6], (DW, FFW), 1.0, 6.0, ((0, 32), (1, 16)))
    moment = scatter_about(keys[7], (DW, FFW), 0.02, 0.12, ((0, 32), (1, 16)), jnp.float32)
    curvature = jnp.clip(jnp.exp(math.log(2.0) - 2.3025851 * jax.random.uniform(keys[8], (DW, FFW), jnp.float32) ** levels(keys[8], (DW, FFW), ((0, 32), (1, 16)), -0.2, 0.2)), 0.2, 2.0)
    step_count = jax.random.randint(keys[9], (), 1, 64).astype(jnp.int32)
    return {"tokens": tokens, "cotangent": cotangent, "gate_weight": gate_weight, "up_weight": up_weight, "probe_gate": probe_gate, "probe_up": probe_up, "probe_down": probe_down, "moment": moment, "curvature": curvature, "step_count": step_count}


CLIP_RMS = 0.5
GAMMA = 0.03
FLOOR = 0.01

def contract_tokens(left_rows, right_rows):
    return lax.dot_general(left_rows, right_rows, (((0,), (0,)), ((), ())), preferred_element_type=jnp.float32)

def swiglu_pair(gate_pre, up_pre, gate_dot, up_dot):
    sigmoid_val = jax.nn.sigmoid(gate_pre)
    silu_val = gate_pre * sigmoid_val
    silu_slope = sigmoid_val * (1.0 + gate_pre * (1.0 - sigmoid_val))
    hidden = (silu_val * up_pre).astype(jnp.bfloat16)
    hidden_dot = (silu_slope * up_pre * gate_dot + silu_val * up_dot).astype(jnp.bfloat16)
    return (hidden, hidden_dot)

def rounded(partial_value):
    narrow = lax.optimization_barrier(partial_value.astype(jnp.bfloat16))
    return narrow.astype(jnp.float32)

def reference(tokens, cotangent, gate_weight, up_weight, probe_gate, probe_up, probe_down, moment, curvature, step_count):
    groups = TOKENS // TOK_DEV
    grouped_tokens = tokens.reshape(groups, TOK_DEV, DW)
    grouped_cot = cotangent.reshape(groups, TOK_DEV, DW)

    def one_group(totals, members):
        group_tok, group_cot = members
        gate_pre = jnp.dot(group_tok, gate_weight, preferred_element_type=jnp.float32)
        up_pre = jnp.dot(group_tok, up_weight, preferred_element_type=jnp.float32)
        gate_dot = jnp.dot(group_tok, probe_gate, preferred_element_type=jnp.float32)
        up_dot = jnp.dot(group_tok, probe_up, preferred_element_type=jnp.float32)
        hidden, hidden_dot = swiglu_pair(gate_pre, up_pre, gate_dot, up_dot)
        grad_part = rounded(contract_tokens(group_cot, hidden) / TOKENS)
        curv_part = rounded(contract_tokens(group_cot, hidden_dot) / TOKENS)
        return ((totals[0] + grad_part, totals[1] + curv_part), None)
    zero_sums = jnp.zeros((DW, FFW), jnp.float32)
    (gradient, hess_vec), leftover = lax.scan(one_group, (zero_sums, zero_sums), (grouped_tokens, grouped_cot))
    norm_total = jnp.sum(gradient * gradient)
    factor = jnp.minimum(1.0, CLIP_RMS * math.sqrt(DW * FFW) / (jnp.sqrt(norm_total) + 1e-06))
    moment_next = 0.96 * moment + 0.04 * (factor * gradient)
    curvature_next = 0.99 * curvature + 0.01 * (probe_down.astype(jnp.float32) * hess_vec)
    step_float = step_count.astype(jnp.float32)
    first_fix = 1.0 - jnp.power(jnp.float32(0.96), step_float)
    second_fix = 1.0 - jnp.power(jnp.float32(0.99), step_float)
    ratio = moment_next / first_fix / jnp.maximum(GAMMA * curvature_next / second_fix, FLOOR)
    direction = jnp.clip(ratio, -1.0, 1.0).astype(jnp.bfloat16)
    return (moment_next, curvature_next, direction)
```

```python
import functools
import math

import jax
import jax.numpy as jnp
from jax import lax
from jax.experimental import pallas as pl
from jax.experimental.pallas import tpu as pltpu
from jax.sharding import Mesh, PartitionSpec as P

DW = 2560
FFW = 6912
TOKENS = 8192

CLIP_RMS = 0.5
GAMMA = 0.03
FLOOR = 0.01

SIZES = (8, 2, 2, 2, 8)
NAMES = ("y", "xl", "core", "xh", "z")
DP = ("y", "xl", "core")
CHIPS = ("y", "xl")
MP = ("xh", "z")

COLUMNS = 256
FORWARD_VMEM = 54 * 1024 * 1024
BACKWARD_VMEM = 16 * 1024 * 1024


def forward_kernel(feat_ref, w_ref, out_ref, tok_ref):
    lines, planes, depth, rows = feat_ref.shape
    half = lines // 2

    @pl.when(pl.program_id(0) == 0)
    def _():
        for part in range(2 * planes):
            first = half * (part % 2)
            piece = feat_ref[first : first + half, part // 2].reshape(half * depth, rows)
            tok_ref[:, part * half * depth : (part + 1) * half * depth] = piece.T

    def project(which):
        piece = w_ref[:, which].reshape(tok_ref.shape[1], w_ref.shape[3])
        return jnp.dot(tok_ref[...], piece, preferred_element_type=jnp.float32)

    gate_pre, up_pre, gate_dot, up_dot = (project(which) for which in range(4))
    sigmoid_val = jax.nn.sigmoid(gate_pre)
    silu_val = gate_pre * sigmoid_val
    silu_slope = sigmoid_val * (1.0 + gate_pre * (1.0 - sigmoid_val))
    out_ref[0] = (silu_val * up_pre).astype(jnp.bfloat16)
    out_ref[1] = (silu_slope * up_pre * gate_dot + silu_val * up_dot).astype(jnp.bfloat16)


def forward(features, weights):
    lines, planes, double, rows = features.shape
    shards, _, depth, units = weights.shape
    width = double // 2
    inputs = lines * planes * width
    return pl.pallas_call(
        forward_kernel,
        out_shape=jax.ShapeDtypeStruct((2, rows, units), jnp.bfloat16),
        grid=(pl.cdiv(units, COLUMNS),),
        in_specs=[
            pl.BlockSpec((lines, planes, width, rows), lambda j: (0, 0, 0, 0)),
            pl.BlockSpec((shards, 4, depth, COLUMNS), lambda j: (0, 0, 0, j)),
        ],
        out_specs=pl.BlockSpec((2, rows, COLUMNS), lambda j: (0, 0, j)),
        scratch_shapes=[pltpu.VMEM((rows, inputs), jnp.bfloat16)],
        compiler_params=pltpu.CompilerParams(vmem_limit_bytes=FORWARD_VMEM),
        cost_estimate=pl.CostEstimate(
            flops=2 * rows * inputs * 4 * units,
            bytes_accessed=weights.size * 2 + inputs * rows * 2,
            transcendentals=rows * units,
        ),
    )(features, weights)


def top_column(block):
    size = jnp.max(jnp.abs(block), axis=0, keepdims=True)
    lane = lax.broadcasted_iota(jnp.int32, size.shape, 1)
    first = jnp.where(size == jnp.max(size, axis=1, keepdims=True), lane, size.shape[1])
    return lane == jnp.min(first, axis=1, keepdims=True)


def rounded_with_rest(block):
    high = block.astype(jnp.bfloat16).astype(jnp.float32)
    rest = jnp.where(top_column(high), block - high, 0.0)
    return high, jnp.sum(rest, axis=1, keepdims=True)


def backward_kernel(cot_ref, mine_ref, other_ref, out_ref):
    blocks, _, double, rows = cot_ref.shape
    depth = double // 2
    sides = []
    for which in range(2):
        piece = cot_ref[:, 0, which * depth : (which + 1) * depth]
        sides.append(piece.reshape(blocks * depth, rows))

    def summed(kind):
        total = 0.0
        for cot, ref in zip(sides, (mine_ref, other_ref)):
            partial = jnp.dot(cot, ref[kind], preferred_element_type=jnp.float32) * (1.0 / TOKENS)
            total += partial.astype(jnp.bfloat16).astype(jnp.float32)
        return total

    totals = [summed(kind) for kind in range(2)]
    for index in range(blocks):
        parts = []
        for total in totals:
            parts += rounded_with_rest(total[index * depth : (index + 1) * depth])
        out_ref[index] = jnp.concatenate(parts, axis=1).astype(jnp.bfloat16)


def backward(features, mine, other):
    lines, planes, double, rows = features.shape
    units = mine.shape[2]
    depth = double // 4
    shards = lines * planes
    parts = 4
    block = shards // parts
    per_plane = parts // planes
    return pl.pallas_call(
        backward_kernel,
        out_shape=jax.ShapeDtypeStruct((shards, depth, 2 * units + 2), jnp.bfloat16),
        grid=(parts,),
        in_specs=[
            pl.BlockSpec(
                (block, 1, double // 2, rows), lambda i: (i % per_plane, i // per_plane, 1, 0)
            ),
            pl.BlockSpec(mine.shape, lambda i: (0, 0, 0)),
            pl.BlockSpec(mine.shape, lambda i: (0, 0, 0)),
        ],
        out_specs=pl.BlockSpec((block, depth, 2 * units + 2), lambda i: (i, 0, 0)),
        compiler_params=pltpu.CompilerParams(vmem_limit_bytes=BACKWARD_VMEM),
        cost_estimate=pl.CostEstimate(
            flops=2 * shards * depth * 4 * rows * units,
            bytes_accessed=2 * (features.size // 2 + 2 * mine.size + shards * depth * 2 * units),
            transcendentals=0,
        ),
    )(features, mine, other)


def gradient_kernel(packed_ref, gradient_ref, square_ref):
    units = gradient_ref.shape[1]
    total = jnp.zeros(gradient_ref.shape, jnp.float32)
    for index in range(packed_ref.shape[0]):
        block = packed_ref[index].astype(jnp.float32)
        high, rest = block[:, :units], block[:, units : units + 1]
        total += high + jnp.where(top_column(high), rest, 0.0)
    gradient_ref[...] = total
    square_ref[...] = jnp.full(square_ref.shape, jnp.sum(total * total))


def gradient_sum(packed, units):
    return pl.pallas_call(
        gradient_kernel,
        out_shape=(
            jax.ShapeDtypeStruct((packed.shape[1], units), jnp.float32),
            jax.ShapeDtypeStruct((1, 128), jnp.float32),
        ),
        compiler_params=pltpu.CompilerParams(vmem_limit_bytes=BACKWARD_VMEM),
    )(packed)


def hessian_kernel(packed_ref, out_ref):
    units = out_ref.shape[1]
    total = jnp.zeros(out_ref.shape, jnp.float32)
    for index in range(packed_ref.shape[0]):
        block = packed_ref[index].astype(jnp.float32)
        high, rest = block[:, units + 1 : 2 * units + 1], block[:, 2 * units + 1 :]
        total += high + jnp.where(top_column(high), rest, 0.0)
    out_ref[...] = total


def hessian_sum(packed, units):
    return pl.pallas_call(
        hessian_kernel,
        out_shape=jax.ShapeDtypeStruct((packed.shape[1], units), jnp.float32),
        compiler_params=pltpu.CompilerParams(vmem_limit_bytes=BACKWARD_VMEM),
    )(packed)


def swap_cores(value):
    return lax.ppermute(value, "core", [(0, 1), (1, 0)])


def to_all(value, axes):
    copies = jnp.broadcast_to(value[None], (lax.axis_size(axes),) + value.shape)
    return lax.all_to_all(copies, axes, 0, 0, tiled=True)


def gather_features(value):
    other = lax.ppermute(value, "xh", [(0, 1), (1, 0)])
    low = lax.axis_index("xh") == 0
    pair = jnp.stack([jnp.where(low, value, other), jnp.where(low, other, value)])
    return to_all(pair, "z")


def sum_over_all(square):
    for axes in (MP, DP):
        square = jnp.sum(to_all(square, axes), axis=0)
    return square[0, 0]


def per_device(
    tokens,
    cotangent,
    gate_weight,
    up_weight,
    probe_gate,
    probe_up,
    probe_down,
    moment,
    curvature,
    step_count,
):
    core = lax.axis_index("core")
    shard_rows, units = gate_weight.shape

    weights = lax.all_gather(
        jnp.stack([gate_weight, up_weight, probe_gate, probe_up]), DP, axis=0, tiled=False
    )
    cot_t = cotangent.T
    cot_mine = lax.dynamic_slice_in_dim(cot_t, core * shard_rows, shard_rows, 0)
    cot_send = lax.dynamic_slice_in_dim(cot_t, (1 - core) * shard_rows, shard_rows, 0)
    features = gather_features(jnp.concatenate([tokens.T, cot_mine, swap_cores(cot_send)]))
    weights, features = lax.optimization_barrier((weights, features))

    hidden = forward(features, weights)
    packed = backward(features, hidden, swap_cores(hidden))
    packed = lax.all_to_all(packed, CHIPS, 0, 0, tiled=True)
    gradient, square = gradient_sum(packed, units)
    norm_total = sum_over_all(square)
    hess_vec = hessian_sum(packed, units)

    factor = jnp.minimum(1.0, CLIP_RMS * math.sqrt(DW * FFW) / (jnp.sqrt(norm_total) + 1e-06))
    moment_next = 0.96 * moment + 0.04 * (factor * gradient)
    curvature_next = 0.99 * curvature + 0.01 * (probe_down.astype(jnp.float32) * hess_vec)
    step_float = step_count.astype(jnp.float32)
    first_fix = 1.0 - jnp.power(jnp.float32(0.96), step_float)
    second_fix = 1.0 - jnp.power(jnp.float32(0.99), step_float)
    ratio = moment_next / first_fix / jnp.maximum(GAMMA * curvature_next / second_fix, FLOOR)
    direction = jnp.clip(ratio, -1.0, 1.0).astype(jnp.bfloat16)
    return (moment_next, curvature_next, direction)


def solution(mesh):
    fine = Mesh(mesh.devices.reshape(SIZES), NAMES)
    block = P(DP, MP)
    return jax.shard_map(
        per_device,
        mesh=fine,
        in_specs=(block,) * 9 + (P(),),
        out_specs=(block,) * 3,
        check_vma=False,
    )
```

```python
import functools
import math

import jax
import jax.numpy as jnp
from jax import lax
from jax.experimental import pallas as pl
from jax.experimental.pallas import tpu as pltpu
from jax.sharding import Mesh, PartitionSpec as P

DW = 2560
FFW = 6912
TOKENS = 8192

CLIP_RMS = 0.5
GAMMA = 0.03
FLOOR = 0.01

SIZES = (8, 2, 2, 2, 8)
NAMES = ("y", "xl", "core", "xh", "z")
DP = ("y", "xl", "core")
CHIPS = ("y", "xl")
MP = ("xh", "z")

COLUMNS = 256
FORWARD_VMEM = 52 * 1024 * 1024
BACKWARD_VMEM = 16 * 1024 * 1024


def forward_kernel(line_ref, feat_ref, w_ref, out_ref, tok_ref):
    lines, planes, depth, rows = feat_ref.shape
    half = lines // 2
    line = line_ref[0]

    @pl.when(pl.program_id(0) == 0)
    def _():
        for part in range(2 * planes):
            first = half * (part % 2)
            pieces = [
                feat_ref[lax.rem(first + step + lines - line, lines), part // 2]
                for step in range(half)
            ]
            piece = jnp.concatenate(pieces, axis=0)
            tok_ref[:, part * half * depth : (part + 1) * half * depth] = piece.T

    def project(which):
        piece = w_ref[:, which].reshape(tok_ref.shape[1], w_ref.shape[3])
        return jnp.dot(tok_ref[...], piece, preferred_element_type=jnp.float32)

    gate_pre, up_pre, gate_dot, up_dot = (project(which) for which in range(4))
    sigmoid_val = jax.nn.sigmoid(gate_pre)
    silu_val = gate_pre * sigmoid_val
    silu_slope = sigmoid_val * (1.0 + gate_pre * (1.0 - sigmoid_val))
    out_ref[0] = (silu_val * up_pre).astype(jnp.bfloat16)
    out_ref[1] = (silu_slope * up_pre * gate_dot + silu_val * up_dot).astype(jnp.bfloat16)


def forward(line, features, weights):
    lines, planes, double, rows = features.shape
    shards, _, depth, units = weights.shape
    width = double // 2
    inputs = lines * planes * width
    return pl.pallas_call(
        forward_kernel,
        out_shape=jax.ShapeDtypeStruct((2, rows, units), jnp.bfloat16),
        grid_spec=pltpu.PrefetchScalarGridSpec(
            num_scalar_prefetch=1,
            grid=(pl.cdiv(units, COLUMNS),),
            in_specs=[
                pl.BlockSpec((lines, planes, width, rows), lambda j, line: (0, 0, 0, 0)),
                pl.BlockSpec((shards, 4, depth, COLUMNS), lambda j, line: (0, 0, 0, j)),
            ],
            out_specs=pl.BlockSpec((2, rows, COLUMNS), lambda j, line: (0, 0, j)),
            scratch_shapes=[pltpu.VMEM((rows, inputs), jnp.bfloat16)],
        ),
        compiler_params=pltpu.CompilerParams(vmem_limit_bytes=FORWARD_VMEM),
        cost_estimate=pl.CostEstimate(
            flops=2 * rows * inputs * 4 * units,
            bytes_accessed=weights.size * 2 + inputs * rows * 2,
            transcendentals=rows * units,
        ),
    )(line, features, weights)


def top_column(block):
    size = jnp.max(jnp.abs(block), axis=0, keepdims=True)
    lane = lax.broadcasted_iota(jnp.int32, size.shape, 1)
    first = jnp.where(size == jnp.max(size, axis=1, keepdims=True), lane, size.shape[1])
    return lane == jnp.min(first, axis=1, keepdims=True)


def rounded_with_rest(block):
    high = block.astype(jnp.bfloat16).astype(jnp.float32)
    rest = jnp.where(top_column(high), block - high, 0.0)
    return high, jnp.sum(rest, axis=1, keepdims=True)


def backward_kernel(line_ref, cot_ref, mine_ref, other_ref, out_ref):
    lines, _, double, _ = cot_ref.shape
    depth = double // 2
    blocks = out_ref.shape[0]
    first = lax.rem(pl.program_id(0), lines // blocks) * blocks + lines - line_ref[0]
    pieces = [cot_ref[lax.rem(first + step, lines), 0] for step in range(blocks)]
    sides = []
    for which in range(2):
        parts = [piece[which * depth : (which + 1) * depth] for piece in pieces]
        sides.append(jnp.concatenate(parts, axis=0))

    def summed(kind):
        total = 0.0
        for cot, ref in zip(sides, (mine_ref, other_ref)):
            partial = jnp.dot(cot, ref[kind], preferred_element_type=jnp.float32) * (1.0 / TOKENS)
            total += partial.astype(jnp.bfloat16).astype(jnp.float32)
        return total

    totals = [summed(kind) for kind in range(2)]
    for index in range(blocks):
        parts = []
        for total in totals:
            parts += rounded_with_rest(total[index * depth : (index + 1) * depth])
        out_ref[index] = jnp.concatenate(parts, axis=1).astype(jnp.bfloat16)


def backward(line, features, mine, other):
    lines, planes, double, rows = features.shape
    units = mine.shape[2]
    depth = double // 4
    shards = lines * planes
    parts = 4
    block = shards // parts
    per_plane = parts // planes
    return pl.pallas_call(
        backward_kernel,
        out_shape=jax.ShapeDtypeStruct((shards, depth, 2 * units + 2), jnp.bfloat16),
        grid_spec=pltpu.PrefetchScalarGridSpec(
            num_scalar_prefetch=1,
            grid=(parts,),
            in_specs=[
                pl.BlockSpec(
                    (lines, 1, double // 2, rows), lambda i, line: (0, i // per_plane, 1, 0)
                ),
                pl.BlockSpec(mine.shape, lambda i, line: (0, 0, 0)),
                pl.BlockSpec(mine.shape, lambda i, line: (0, 0, 0)),
            ],
            out_specs=pl.BlockSpec((block, depth, 2 * units + 2), lambda i, line: (i, 0, 0)),
        ),
        compiler_params=pltpu.CompilerParams(vmem_limit_bytes=BACKWARD_VMEM),
        cost_estimate=pl.CostEstimate(
            flops=2 * shards * depth * 4 * rows * units,
            bytes_accessed=2 * (features.size // 2 + 2 * mine.size + shards * depth * 2 * units),
            transcendentals=0,
        ),
    )(line, features, mine, other)


def gradient_kernel(packed_ref, gradient_ref, square_ref):
    units = gradient_ref.shape[1]
    total = jnp.zeros(gradient_ref.shape, jnp.float32)
    for index in range(packed_ref.shape[0]):
        block = packed_ref[index].astype(jnp.float32)
        high, rest = block[:, :units], block[:, units : units + 1]
        total += high + jnp.where(top_column(high), rest, 0.0)
    gradient_ref[...] = total
    square_ref[...] = jnp.full(square_ref.shape, jnp.sum(total * total))


def gradient_sum(packed, units):
    return pl.pallas_call(
        gradient_kernel,
        out_shape=(
            jax.ShapeDtypeStruct((packed.shape[1], units), jnp.float32),
            jax.ShapeDtypeStruct((1, 128), jnp.float32),
        ),
        compiler_params=pltpu.CompilerParams(vmem_limit_bytes=BACKWARD_VMEM),
    )(packed)


def hessian_kernel(packed_ref, out_ref):
    units = out_ref.shape[1]
    total = jnp.zeros(out_ref.shape, jnp.float32)
    for index in range(packed_ref.shape[0]):
        block = packed_ref[index].astype(jnp.float32)
        high, rest = block[:, units + 1 : 2 * units + 1], block[:, 2 * units + 1 :]
        total += high + jnp.where(top_column(high), rest, 0.0)
    out_ref[...] = total


def hessian_sum(packed, units):
    return pl.pallas_call(
        hessian_kernel,
        out_shape=jax.ShapeDtypeStruct((packed.shape[1], units), jnp.float32),
        compiler_params=pltpu.CompilerParams(vmem_limit_bytes=BACKWARD_VMEM),
    )(packed)


def swap_cores(value):
    return lax.ppermute(value, "core", [(0, 1), (1, 0)])


def to_all(value, axes):
    copies = jnp.broadcast_to(value[None], (lax.axis_size(axes),) + value.shape)
    return lax.all_to_all(copies, axes, 0, 0, tiled=True)


def pair_features(value):
    other = lax.ppermute(value, "xh", [(0, 1), (1, 0)])
    low = lax.axis_index("xh") == 0
    return jnp.stack([jnp.where(low, value, other), jnp.where(low, other, value)])


def ring_gather(value):
    lines = lax.axis_size("z")
    up = [(place, (place + 1) % lines) for place in range(lines)]
    down = [(to, start) for start, to in up]
    below, above = [value], [value]
    for _ in range(lines // 2 - 1):
        below.append(lax.ppermute(below[-1], "z", up))
        above.append(lax.ppermute(above[-1], "z", down))
    first = lax.ppermute(below[-1][0], "z", up)
    second = lax.ppermute(above[-1][1], "z", down)
    return jnp.stack(above + [jnp.stack([first, second])] + below[:0:-1])


def sum_over_all(square):
    for axes in (MP, DP):
        square = jnp.sum(to_all(square, axes), axis=0)
    return square[0, 0]


def per_device(
    tokens,
    cotangent,
    gate_weight,
    up_weight,
    probe_gate,
    probe_up,
    probe_down,
    moment,
    curvature,
    step_count,
):
    core = lax.axis_index("core")
    shard_rows, units = gate_weight.shape

    weights = lax.all_gather(
        jnp.stack([gate_weight, up_weight, probe_gate, probe_up]), DP, axis=0, tiled=False
    )
    cot_t = cotangent.T
    cot_mine = lax.dynamic_slice_in_dim(cot_t, core * shard_rows, shard_rows, 0)
    cot_send = lax.dynamic_slice_in_dim(cot_t, (1 - core) * shard_rows, shard_rows, 0)
    mine = jnp.concatenate([tokens.T, cot_mine, swap_cores(cot_send)])
    features = ring_gather(pair_features(mine))
    weights, features = lax.optimization_barrier((weights, features))

    line = lax.axis_index("z").reshape(1)
    hidden = forward(line, features, weights)
    packed = backward(line, features, hidden, swap_cores(hidden))
    packed = lax.all_to_all(packed, CHIPS, 0, 0, tiled=True)
    gradient, square = gradient_sum(packed, units)
    norm_total = sum_over_all(square)
    hess_vec = hessian_sum(packed, units)

    factor = jnp.minimum(1.0, CLIP_RMS * math.sqrt(DW * FFW) / (jnp.sqrt(norm_total) + 1e-06))
    moment_next = 0.96 * moment + 0.04 * (factor * gradient)
    curvature_next = 0.99 * curvature + 0.01 * (probe_down.astype(jnp.float32) * hess_vec)
    step_float = step_count.astype(jnp.float32)
    first_fix = 1.0 - jnp.power(jnp.float32(0.96), step_float)
    second_fix = 1.0 - jnp.power(jnp.float32(0.99), step_float)
    ratio = moment_next / first_fix / jnp.maximum(GAMMA * curvature_next / second_fix, FLOOR)
    direction = jnp.clip(ratio, -1.0, 1.0).astype(jnp.bfloat16)
    return (moment_next, curvature_next, direction)


def solution(mesh):
    fine = Mesh(mesh.devices.reshape(SIZES), NAMES)
    block = P(DP, MP)
    return jax.shard_map(
        per_device,
        mesh=fine,
        in_specs=(block,) * 9 + (P(),),
        out_specs=(block,) * 3,
        check_vma=False,
    )
```

```python
import functools
import math

import jax
import jax.numpy as jnp
from jax import lax
from jax.experimental import pallas as pl
from jax.experimental.pallas import tpu as pltpu
from jax.sharding import Mesh, PartitionSpec as P

DW = 2560
FFW = 6912
TOKENS = 8192

CLIP_RMS = 0.5
GAMMA = 0.03
FLOOR = 0.01

SIZES = (8, 2, 2, 2, 8)
NAMES = ("y", "xl", "core", "xh", "z")
DP = ("y", "xl", "core")
CHIPS = ("y", "xl")
MP = ("xh", "z")

COLUMNS = 256
PADDED = 48
FORWARD_VMEM = 52 * 1024 * 1024
BACKWARD_VMEM = 24 * 1024 * 1024


def forward_kernel(line_ref, feat_ref, w_ref, out_ref, tok_ref):
    lines, planes, _, rows = feat_ref.shape
    half = lines // 2
    depth = tok_ref.shape[1] // (lines * planes)
    line = line_ref[0]

    @pl.when(pl.program_id(0) == 0)
    def _():
        for part in range(2 * planes):
            first = half * (part % 2)
            pieces = [
                feat_ref[lax.rem(first + step + lines - line, lines), part // 2, :depth]
                for step in range(half)
            ]
            piece = jnp.concatenate(pieces, axis=0)
            tok_ref[:, part * half * depth : (part + 1) * half * depth] = piece.T

    def project(which):
        piece = w_ref[:, which].reshape(tok_ref.shape[1], w_ref.shape[3])
        return jnp.dot(tok_ref[...], piece, preferred_element_type=jnp.float32)

    gate_pre, up_pre, gate_dot, up_dot = (project(which) for which in range(4))
    sigmoid_val = jax.nn.sigmoid(gate_pre)
    silu_val = gate_pre * sigmoid_val
    silu_slope = sigmoid_val * (1.0 + gate_pre * (1.0 - sigmoid_val))
    out_ref[0] = (silu_val * up_pre).astype(jnp.bfloat16)
    out_ref[1] = (silu_slope * up_pre * gate_dot + silu_val * up_dot).astype(jnp.bfloat16)


def forward(line, features, weights):
    lines, planes, _, rows = features.shape
    shards, _, depth, units = weights.shape
    inputs = shards * depth
    return pl.pallas_call(
        forward_kernel,
        out_shape=jax.ShapeDtypeStruct((2, rows, units), jnp.bfloat16),
        grid_spec=pltpu.PrefetchScalarGridSpec(
            num_scalar_prefetch=1,
            grid=(pl.cdiv(units, COLUMNS),),
            in_specs=[
                pl.BlockSpec(features.shape, lambda j, line: (0, 0, 0, 0)),
                pl.BlockSpec((shards, 4, depth, COLUMNS), lambda j, line: (0, 0, 0, j)),
            ],
            out_specs=pl.BlockSpec((2, rows, COLUMNS), lambda j, line: (0, 0, j)),
            scratch_shapes=[pltpu.VMEM((rows, inputs), jnp.bfloat16)],
        ),
        compiler_params=pltpu.CompilerParams(vmem_limit_bytes=FORWARD_VMEM),
        cost_estimate=pl.CostEstimate(
            flops=2 * rows * inputs * 4 * units,
            bytes_accessed=weights.size * 2 + inputs * rows * 2,
            transcendentals=rows * units,
        ),
    )(line, features, weights)


def top_column(block):
    size = jnp.max(jnp.abs(block), axis=0, keepdims=True)
    lane = lax.broadcasted_iota(jnp.int32, size.shape, 1)
    first = jnp.where(size == jnp.max(size, axis=1, keepdims=True), lane, size.shape[1])
    return lane == jnp.min(first, axis=1, keepdims=True)


def rounded_with_rest(block):
    high = block.astype(jnp.bfloat16).astype(jnp.float32)
    rest = jnp.where(top_column(high), block - high, 0.0)
    return high, jnp.sum(rest, axis=1, keepdims=True)


def backward_kernel(line_ref, feat_ref, *refs):
    out_ref, groups = refs[-1], refs[:-1]
    lines, _, width, _ = feat_ref.shape
    start = width - len(groups) * PADDED
    first = lines - line_ref[0]
    pieces = [feat_ref[lax.rem(first + step, lines), 0] for step in range(lines)]

    def summed(kind):
        total = 0.0
        for index, ref in enumerate(groups):
            begin = start + index * PADDED
            cot = jnp.concatenate([piece[begin : begin + PADDED] for piece in pieces], axis=0)
            partial = jnp.dot(cot, ref[kind], preferred_element_type=jnp.float32) * (1.0 / TOKENS)
            total += partial.astype(jnp.bfloat16).astype(jnp.float32)
        return total

    totals = [summed(kind) for kind in range(2)]
    for index in range(lines):
        begin = index * PADDED
        parts = []
        for total in totals:
            parts += rounded_with_rest(total[begin : begin + out_ref.shape[1]])
        out_ref[index] = jnp.concatenate(parts, axis=1).astype(jnp.bfloat16)


def backward(line, features, groups, depth):
    lines, planes, width, rows = features.shape
    units = groups[0].shape[2]
    shards = lines * planes
    hidden_spec = pl.BlockSpec(groups[0].shape, lambda i, line: (0, 0, 0))
    return pl.pallas_call(
        backward_kernel,
        out_shape=jax.ShapeDtypeStruct((shards, depth, 2 * units + 2), jnp.bfloat16),
        grid_spec=pltpu.PrefetchScalarGridSpec(
            num_scalar_prefetch=1,
            grid=(planes,),
            in_specs=[
                pl.BlockSpec((lines, 1, width, rows), lambda i, line: (0, i, 0, 0)),
                *[hidden_spec for _ in groups],
            ],
            out_specs=pl.BlockSpec((lines, depth, 2 * units + 2), lambda i, line: (i, 0, 0)),
        ),
        compiler_params=pltpu.CompilerParams(vmem_limit_bytes=BACKWARD_VMEM),
        cost_estimate=pl.CostEstimate(
            flops=2 * shards * PADDED * len(groups) * rows * 2 * units,
            bytes_accessed=2 * (features.size + 4 * groups[0].size + shards * depth * 2 * units),
            transcendentals=0,
        ),
    )(line, features, *groups)


def add_up(packed_ref, out_ref, begin):
    depth = packed_ref.shape[1]
    units = out_ref.shape[1]
    for side in range(2):
        total = jnp.zeros((depth, units), jnp.float32)
        for index in range(side, packed_ref.shape[0], 2):
            block = packed_ref[index].astype(jnp.float32)
            high = block[:, begin : begin + units]
            rest = block[:, begin + units : begin + units + 1]
            total += high + jnp.where(top_column(high), rest, 0.0)
        out_ref[side * depth : (side + 1) * depth] = total


def gradient_kernel(packed_ref, gradient_ref, square_ref):
    add_up(packed_ref, gradient_ref, 0)
    total = gradient_ref[...]
    square_ref[...] = jnp.full(square_ref.shape, jnp.sum(total * total))


def gradient_sum(packed, units):
    return pl.pallas_call(
        gradient_kernel,
        out_shape=(
            jax.ShapeDtypeStruct((2 * packed.shape[1], units), jnp.float32),
            jax.ShapeDtypeStruct((1, 128), jnp.float32),
        ),
        compiler_params=pltpu.CompilerParams(vmem_limit_bytes=BACKWARD_VMEM),
    )(packed)


def hessian_kernel(packed_ref, out_ref):
    add_up(packed_ref, out_ref, out_ref.shape[1] + 1)


def hessian_sum(packed, units):
    return pl.pallas_call(
        hessian_kernel,
        out_shape=jax.ShapeDtypeStruct((2 * packed.shape[1], units), jnp.float32),
        compiler_params=pltpu.CompilerParams(vmem_limit_bytes=BACKWARD_VMEM),
    )(packed)


def swap(value, axis):
    return lax.ppermute(value, axis, [(0, 1), (1, 0)])


def share(value, axis):
    place = lax.axis_index(axis)
    mine = lax.dynamic_index_in_dim(value, place, 0, keepdims=False)
    send = lax.dynamic_index_in_dim(value, 1 - place, 0, keepdims=False)
    return jnp.stack([mine, swap(send, axis)])


def to_all(value, axes):
    copies = jnp.broadcast_to(value[None], (lax.axis_size(axes),) + value.shape)
    return lax.all_to_all(copies, axes, 0, 0, tiled=True)


def pair_features(value):
    other = swap(value, "xh")
    low = lax.axis_index("xh") == 0
    return jnp.stack([jnp.where(low, value, other), jnp.where(low, other, value)])


def ring_gather(value):
    lines = lax.axis_size("z")
    up = [(place, (place + 1) % lines) for place in range(lines)]
    down = [(to, start) for start, to in up]
    below, above = [value], [value]
    for _ in range(lines // 2 - 1):
        below.append(lax.ppermute(below[-1], "z", up))
        above.append(lax.ppermute(above[-1], "z", down))
    first = lax.ppermute(below[-1][0], "z", up)
    second = lax.ppermute(above[-1][1], "z", down)
    return jnp.stack(above + [jnp.stack([first, second])] + below[:0:-1])


def sum_over_all(square):
    for axes in (MP, DP):
        square = jnp.sum(to_all(square, axes), axis=0)
    return square[0, 0]


def per_device(
    tokens,
    cotangent,
    gate_weight,
    up_weight,
    probe_gate,
    probe_up,
    probe_down,
    moment,
    curvature,
    step_count,
):
    shard_rows, units = gate_weight.shape

    weights = lax.all_gather(
        jnp.stack([gate_weight, up_weight, probe_gate, probe_up]), DP, axis=0, tiled=False
    )
    rows = tokens.shape[0]
    depth = shard_rows // 2
    cot = cotangent.T.reshape(2, 2, depth, rows).swapaxes(0, 1)
    cot = share(share(cot, "xl").swapaxes(0, 1), "core")
    cot = jnp.pad(cot, ((0, 0), (0, 0), (0, PADDED - depth), (0, 0))).reshape(-1, rows)
    features = ring_gather(pair_features(jnp.concatenate([tokens.T, cot])))
    weights, features = lax.optimization_barrier((weights, features))

    line = lax.axis_index("z").reshape(1)
    hidden = forward(line, features, weights)
    far = swap(hidden, "xl")
    groups = (hidden, far, swap(hidden, "core"), swap(far, "core"))
    packed = backward(line, features, groups, depth)
    packed = lax.all_to_all(packed, CHIPS, 0, 0, tiled=True)
    gradient, square = gradient_sum(packed, units)
    norm_total = sum_over_all(square)
    hess_vec = hessian_sum(packed, units)

    factor = jnp.minimum(1.0, CLIP_RMS * math.sqrt(DW * FFW) / (jnp.sqrt(norm_total) + 1e-06))
    moment_next = 0.96 * moment + 0.04 * (factor * gradient)
    curvature_next = 0.99 * curvature + 0.01 * (probe_down.astype(jnp.float32) * hess_vec)
    step_float = step_count.astype(jnp.float32)
    first_fix = 1.0 - jnp.power(jnp.float32(0.96), step_float)
    second_fix = 1.0 - jnp.power(jnp.float32(0.99), step_float)
    ratio = moment_next / first_fix / jnp.maximum(GAMMA * curvature_next / second_fix, FLOOR)
    direction = jnp.clip(ratio, -1.0, 1.0).astype(jnp.bfloat16)
    return (moment_next, curvature_next, direction)


def solution(mesh):
    fine = Mesh(mesh.devices.reshape(SIZES), NAMES)
    block = P(DP, MP)
    return jax.shard_map(
        per_device,
        mesh=fine,
        in_specs=(block,) * 9 + (P(),),
        out_specs=(block,) * 3,
        check_vma=False,
    )
```

```python
import functools
import math

import jax
import jax.numpy as jnp
from jax import lax
from jax.experimental import pallas as pl
from jax.experimental.pallas import tpu as pltpu
from jax.sharding import Mesh, PartitionSpec as P

DW = 2560
FFW = 6912
TOKENS = 8192

CLIP_RMS = 0.5
GAMMA = 0.03
FLOOR = 0.01

SIZES = (8, 2, 2, 2, 8)
NAMES = ("y", "xl", "core", "xh", "z")
DP = ("y", "xl", "core")
CHIPS = ("y", "xl")
MP = ("xh", "z")

COLUMNS = 256
PADDED = 48
FORWARD_VMEM = 52 * 1024 * 1024
BACKWARD_VMEM = 24 * 1024 * 1024


def forward_kernel(line_ref, feat_ref, w_ref, out_ref, tok_ref):
    lines, planes, _, rows = feat_ref.shape
    half = lines // 2
    depth = tok_ref.shape[1] // (lines * planes)
    line = line_ref[0]

    @pl.when(pl.program_id(0) == 0)
    def _():
        for part in range(2 * planes):
            first = half * (part % 2)
            pieces = [
                feat_ref[lax.rem(first + step + lines - line, lines), part // 2, :depth]
                for step in range(half)
            ]
            piece = jnp.concatenate(pieces, axis=0)
            tok_ref[:, part * half * depth : (part + 1) * half * depth] = piece.T

    def project(which):
        piece = w_ref[:, which].reshape(tok_ref.shape[1], w_ref.shape[3])
        return jnp.dot(tok_ref[...], piece, preferred_element_type=jnp.float32)

    gate_pre, up_pre, gate_dot, up_dot = (project(which) for which in range(4))
    sigmoid_val = jax.nn.sigmoid(gate_pre)
    silu_val = gate_pre * sigmoid_val
    silu_slope = sigmoid_val * (1.0 + gate_pre * (1.0 - sigmoid_val))
    out_ref[0] = (silu_val * up_pre).astype(jnp.bfloat16).T
    out_ref[1] = (silu_slope * up_pre * gate_dot + silu_val * up_dot).astype(jnp.bfloat16).T


def forward(line, features, weights):
    lines, planes, _, rows = features.shape
    shards, _, depth, units = weights.shape
    inputs = shards * depth
    return pl.pallas_call(
        forward_kernel,
        out_shape=jax.ShapeDtypeStruct((2, units, rows), jnp.bfloat16),
        grid_spec=pltpu.PrefetchScalarGridSpec(
            num_scalar_prefetch=1,
            grid=(pl.cdiv(units, COLUMNS),),
            in_specs=[
                pl.BlockSpec(features.shape, lambda j, line: (0, 0, 0, 0)),
                pl.BlockSpec((shards, 4, depth, COLUMNS), lambda j, line: (0, 0, 0, j)),
            ],
            out_specs=pl.BlockSpec((2, COLUMNS, rows), lambda j, line: (0, j, 0)),
            scratch_shapes=[pltpu.VMEM((rows, inputs), jnp.bfloat16)],
        ),
        compiler_params=pltpu.CompilerParams(vmem_limit_bytes=FORWARD_VMEM),
        cost_estimate=pl.CostEstimate(
            flops=2 * rows * inputs * 4 * units,
            bytes_accessed=weights.size * 2 + inputs * rows * 2,
            transcendentals=rows * units,
        ),
    )(line, features, weights)


def top_column(block):
    size = jnp.max(jnp.abs(block), axis=0, keepdims=True)
    lane = lax.broadcasted_iota(jnp.int32, size.shape, 1)
    first = jnp.where(size == jnp.max(size, axis=1, keepdims=True), lane, size.shape[1])
    return lane == jnp.min(first, axis=1, keepdims=True)


def rounded_with_rest(block):
    high = block.astype(jnp.bfloat16).astype(jnp.float32)
    rest = jnp.where(top_column(high), block - high, 0.0)
    return high, jnp.sum(rest, axis=1, keepdims=True)


def against_rows(left, right):
    return lax.dot_general(
        left, right, (((1,), (1,)), ((), ())), preferred_element_type=jnp.float32
    )


def backward_kernel(line_ref, feat_ref, *refs):
    out_ref, groups = refs[-1], refs[:-1]
    lines, _, width, _ = feat_ref.shape
    start = width - len(groups) * PADDED
    first = lines - line_ref[0]
    pieces = [feat_ref[lax.rem(first + step, lines), 0] for step in range(lines)]

    def summed(kind):
        total = 0.0
        for index, ref in enumerate(groups):
            begin = start + index * PADDED
            cot = jnp.concatenate([piece[begin : begin + PADDED] for piece in pieces], axis=0)
            partial = against_rows(cot, ref[kind]) * (1.0 / TOKENS)
            total += partial.astype(jnp.bfloat16).astype(jnp.float32)
        return total

    totals = [summed(kind) for kind in range(2)]
    for index in range(lines):
        begin = index * PADDED
        parts = []
        for total in totals:
            parts += rounded_with_rest(total[begin : begin + out_ref.shape[1]])
        out_ref[index] = jnp.concatenate(parts, axis=1).astype(jnp.bfloat16)


def backward(line, features, groups, depth):
    lines, planes, width, rows = features.shape
    units = groups[0].shape[1]
    shards = lines * planes
    hidden_spec = pl.BlockSpec(groups[0].shape, lambda i, line: (0, 0, 0))
    return pl.pallas_call(
        backward_kernel,
        out_shape=jax.ShapeDtypeStruct((shards, depth, 2 * units + 2), jnp.bfloat16),
        grid_spec=pltpu.PrefetchScalarGridSpec(
            num_scalar_prefetch=1,
            grid=(planes,),
            in_specs=[
                pl.BlockSpec((lines, 1, width, rows), lambda i, line: (0, i, 0, 0)),
                *[hidden_spec for _ in groups],
            ],
            out_specs=pl.BlockSpec((lines, depth, 2 * units + 2), lambda i, line: (i, 0, 0)),
        ),
        compiler_params=pltpu.CompilerParams(vmem_limit_bytes=BACKWARD_VMEM),
        cost_estimate=pl.CostEstimate(
            flops=2 * shards * PADDED * len(groups) * rows * 2 * units,
            bytes_accessed=2 * (features.size + 4 * groups[0].size + shards * depth * 2 * units),
            transcendentals=0,
        ),
    )(line, features, *groups)


def add_up(packed_ref, out_ref, begin):
    depth = packed_ref.shape[1]
    units = out_ref.shape[1]
    for side in range(2):
        total = jnp.zeros((depth, units), jnp.float32)
        for index in range(side, packed_ref.shape[0], 2):
            block = packed_ref[index].astype(jnp.float32)
            high = block[:, begin : begin + units]
            rest = block[:, begin + units : begin + units + 1]
            total += high + jnp.where(top_column(high), rest, 0.0)
        out_ref[side * depth : (side + 1) * depth] = total


def gradient_kernel(packed_ref, gradient_ref, square_ref):
    add_up(packed_ref, gradient_ref, 0)
    total = gradient_ref[...]
    square_ref[...] = jnp.full(square_ref.shape, jnp.sum(total * total))


def gradient_sum(packed, units):
    return pl.pallas_call(
        gradient_kernel,
        out_shape=(
            jax.ShapeDtypeStruct((2 * packed.shape[1], units), jnp.float32),
            jax.ShapeDtypeStruct((1, 128), jnp.float32),
        ),
        compiler_params=pltpu.CompilerParams(vmem_limit_bytes=BACKWARD_VMEM),
    )(packed)


def hessian_kernel(packed_ref, out_ref):
    add_up(packed_ref, out_ref, out_ref.shape[1] + 1)


def hessian_sum(packed, units):
    return pl.pallas_call(
        hessian_kernel,
        out_shape=jax.ShapeDtypeStruct((2 * packed.shape[1], units), jnp.float32),
        compiler_params=pltpu.CompilerParams(vmem_limit_bytes=BACKWARD_VMEM),
    )(packed)


def swap(value, axis):
    return lax.ppermute(value, axis, [(0, 1), (1, 0)])


def share(value, axis):
    place = lax.axis_index(axis)
    mine = lax.dynamic_index_in_dim(value, place, 0, keepdims=False)
    send = lax.dynamic_index_in_dim(value, 1 - place, 0, keepdims=False)
    return jnp.stack([mine, swap(send, axis)])


def to_all(value, axes):
    copies = jnp.broadcast_to(value[None], (lax.axis_size(axes),) + value.shape)
    return lax.all_to_all(copies, axes, 0, 0, tiled=True)


def pair_features(value):
    other = swap(value, "xh")
    low = lax.axis_index("xh") == 0
    return jnp.stack([jnp.where(low, value, other), jnp.where(low, other, value)])


def ring_gather(value):
    lines = lax.axis_size("z")
    up = [(place, (place + 1) % lines) for place in range(lines)]
    down = [(to, start) for start, to in up]
    below, above = [value], [value]
    for _ in range(lines // 2 - 1):
        below.append(lax.ppermute(below[-1], "z", up))
        above.append(lax.ppermute(above[-1], "z", down))
    first = lax.ppermute(below[-1][0], "z", up)
    second = lax.ppermute(above[-1][1], "z", down)
    return jnp.stack(above + [jnp.stack([first, second])] + below[:0:-1])


def sum_over_all(square):
    for axes in (MP, DP):
        square = jnp.sum(to_all(square, axes), axis=0)
    return square[0, 0]


def per_device(
    tokens,
    cotangent,
    gate_weight,
    up_weight,
    probe_gate,
    probe_up,
    probe_down,
    moment,
    curvature,
    step_count,
):
    shard_rows, units = gate_weight.shape

    weights = lax.all_gather(
        jnp.stack([gate_weight, up_weight, probe_gate, probe_up]), DP, axis=0, tiled=False
    )
    rows = tokens.shape[0]
    depth = shard_rows // 2
    cot = cotangent.T.reshape(2, 2, depth, rows).swapaxes(0, 1)
    cot = share(share(cot, "xl").swapaxes(0, 1), "core")
    cot = jnp.pad(cot, ((0, 0), (0, 0), (0, PADDED - depth), (0, 0))).reshape(-1, rows)
    features = ring_gather(pair_features(jnp.concatenate([tokens.T, cot])))
    weights, features = lax.optimization_barrier((weights, features))

    line = lax.axis_index("z").reshape(1)
    hidden = forward(line, features, weights)
    far = swap(hidden, "xl")
    groups = (hidden, far, swap(hidden, "core"), swap(far, "core"))
    packed = backward(line, features, groups, depth)
    packed = lax.all_to_all(packed, CHIPS, 0, 0, tiled=True)
    gradient, square = gradient_sum(packed, units)
    norm_total = sum_over_all(square)
    hess_vec = hessian_sum(packed, units)

    factor = jnp.minimum(1.0, CLIP_RMS * math.sqrt(DW * FFW) / (jnp.sqrt(norm_total) + 1e-06))
    moment_next = 0.96 * moment + 0.04 * (factor * gradient)
    curvature_next = 0.99 * curvature + 0.01 * (probe_down.astype(jnp.float32) * hess_vec)
    step_float = step_count.astype(jnp.float32)
    first_fix = 1.0 - jnp.power(jnp.float32(0.96), step_float)
    second_fix = 1.0 - jnp.power(jnp.float32(0.99), step_float)
    ratio = moment_next / first_fix / jnp.maximum(GAMMA * curvature_next / second_fix, FLOOR)
    direction = jnp.clip(ratio, -1.0, 1.0).astype(jnp.bfloat16)
    return (moment_next, curvature_next, direction)


def solution(mesh):
    fine = Mesh(mesh.devices.reshape(SIZES), NAMES)
    block = P(DP, MP)
    return jax.shard_map(
        per_device,
        mesh=fine,
        in_specs=(block,) * 9 + (P(),),
        out_specs=(block,) * 3,
        check_vma=False,
    )
```
